512 devices in a mesh: depth: 4 (over y_lo, core), rows: 8 (over y_hi, x), cols: 16 (over z).
Axes of the slice: x: 4, y: 4 (y_hi: 2, y_lo: 2; y = y_hi * 2 + y_lo), z: 16, core: 2. Of those that a mesh axis runs over, the one named last changes fastest.
Arguments:
- voltage: float32 [16, 128, 2048], P('depth', 'rows', 'cols'), may hold values from -6 to 6
- states: float32 [16, 128, 41, 2048], P('depth', 'rows', None, 'cols'), may hold values from 0 to 1
- cell_tags: int32 [16, 128, 2048], P('depth', 'rows', 'cols'), may hold values from 0 to 2, as said below
- fibre_ids: int32 [16, 128, 2048], P('depth', 'rows', 'cols'), may hold values from 0 to 7
- loan_states: float32 [512, 16, 4, 41, 128], P(('depth', 'rows', 'cols')), may hold values from 0 to 1
- loan_tags: int32 [512, 16, 4, 128], P(('depth', 'rows', 'cols')), may hold values from 0 to 2, as said below
- lend_block: int32 [512, 16, 4], P(('depth', 'rows', 'cols')), may hold values from 0 to 63, as said below
- lend_count: int32 [512, 16], P(('depth', 'rows', 'cols')), may hold values from 0 to 4, as said below
- diffuse_main: float32 [3, 8], replicated, may hold values from 0.02 to 0.08
- diffuse_cross: float32 [3, 8], replicated, may hold values from -0.02 to 0.02
- gate_half: float32 [3, 41], replicated, may hold values from -1 to 1
- gate_slope: float32 [3, 41], replicated, may hold values from 0.2 to 1
- gate_rate: float32 [3, 41], replicated, may hold values from 0.05 to 3
- conductance: float32 [3, 41], replicated, may hold values from -1 to 1
- reversal: float32 [3, 41], replicated, may hold values from -1 to 1
Outputs:
- voltage_out: float32 [16, 128, 2048], P('depth', 'rows', 'cols')
- states_out: float32 [16, 128, 41, 2048], P('depth', 'rows', None, 'cols')
The draws below stay inside these ranges and needn't reach their ends.
Inputs may be any that keep to these rules, and one draw needn't show every extreme that they name: `cell_tags`: column c of a voxel's device decides its mix: columns below 8 are mostly ventricle, the others mostly atrium and scar. `loan_tags`: mostly ventricle. `lend_block`: for each device, its 64 block ids are all different. `lend_count`: nonzero only where the device's column c is below 8 and the lender column is not; for such a device column c + 8 gets exactly 4.
All inputs are finite; a program needn't handle non-finite values.
Results may differ from the reference program's by a relative error of at most 0.0003.
Values sent between devices are 32-bit elements; how exact they have to be, the bound alone decides.
No kernel may reach another device: no remote copies, remote signals or barrier semaphores. Data moves between devices by JAX's collectives and lax.ppermute only.
A program may use at most 64 MiB of HBM per device.

```python
import math
import jax
import jax.numpy as jnp
from jax import lax

STATES = 41
ATRIAL = 21
SCAR = 5
REGIONS = 8
STEPS = 2
CX = 4
CY = 16
CZ = 128
CAP = 4
NX = 16
NY = 128
NZ = 2048
N_DEPTH = 4
N_ROWS = 8
N_COLS = 16


def lend_plan(key):
    keys = jax.random.split(key, N_DEPTH * N_ROWS * N_COLS)

    def pick_blocks(one_key):
        return jax.random.permutation(one_key, CX * CY)[:N_COLS * CAP]
    blocks = jax.vmap(pick_blocks)(keys).reshape(N_DEPTH * N_ROWS * N_COLS, N_COLS, CAP)
    counts = jax.random.randint(jax.random.fold_in(key, 11), (N_DEPTH * N_ROWS * N_COLS, N_COLS), 0, CAP + 1)
    own_col = jnp.arange(N_DEPTH * N_ROWS * N_COLS) % N_COLS
    columns = jnp.arange(N_COLS)
    half_cols = N_COLS // 2
    heavy = (own_col < half_cols)[:, None]
    light_target = (columns >= half_cols)[None, :]
    counts = jnp.where(heavy & light_target, counts, 0)
    counts = jnp.where(heavy & (columns[None, :] == (own_col + half_cols)[:, None]), CAP, counts)
    return (blocks.astype(jnp.int32), counts.astype(jnp.int32))


def draw_lend_block(key, part):
    return lend_plan(key)[0]


def draw_lend_count(key, part):
    return lend_plan(key)[1]


def draw_cell_tags(key, part):
    key = jax.random.fold_in(key, 21)
    level = jax.random.randint(key, (NX, NY, NZ), 0, 20)
    column = jnp.arange(NZ, dtype=jnp.int32) // CZ
    heavy = (column < N_COLS // 2)[None, None, :]
    heavy_tag = jnp.where(level < 16, 0, jnp.where(level < 19, 1, 2))
    light_tag = jnp.where(level < 3, 0, jnp.where(level < 12, 1, 2))
    return jnp.where(heavy, heavy_tag, light_tag).astype(jnp.int32)


def draw_loan_tags(key, part):
    key = jax.random.fold_in(key, 23)
    level = jax.random.randint(key, (N_DEPTH * N_ROWS * N_COLS, N_COLS, CAP, CZ), 0, 20)
    return jnp.where(level < 16, 0, jnp.where(level < 19, 1, 2)).astype(jnp.int32)


def set_ends(values, stream_key, smallest, high):
    dims = values.shape
    place = [jax.random.randint(jax.random.fold_in(stream_key, axis), (), 0, dims[axis]) for axis in range(len(dims))]
    values = values.at[tuple(place)].set(smallest)
    longest = dims.index(max(dims))
    place[longest] = (place[longest] + 1) % dims[longest]
    return values.at[tuple(place)].set(high)


def shard_levels(own_key, extent, cuts, least, top_value):
    loudness = 1.0
    for axis_at, parts in cuts:
        steps = jax.random.uniform(jax.random.fold_in(jax.random.fold_in(own_key, 6), axis_at), (parts,), jnp.float32, least / len(cuts), top_value / len(cuts))
        loudness = loudness * jnp.repeat(jnp.exp(steps), extent[axis_at] // parts).reshape((-1,) + (1,) * (len(extent) - 1 - axis_at))
    return loudness


def gaussian(rng, shape, deviation, reach, cuts=(), held_as=jnp.bfloat16):
    values = jax.random.normal(rng, shape, jnp.float32) * deviation
    if len(cuts) > 0:
        values = shard_levels(rng, shape, cuts, -0.22, 0.18) * values
    return jnp.clip(values, min=-reach, max=reach).astype(held_as)


def setup_inputs(seed: int = 0) -> dict:
    streams_of = jax.random.split(jax.random.key(seed), 16)
    voltage = gaussian(streams_of[0], (NX, NY, NZ), 1.0, 6.0, ((0, 4), (1, 8), (2, 16)), jnp.float32)
    states = jnp.clip(1.0 * jax.random.uniform(streams_of[1], (NX, NY, STATES, NZ), jnp.float32) ** shard_levels(streams_of[1], (NX, NY, STATES, NZ), ((0, 4), (1, 8), (3, 16)), -0.2, 0.2), 0.0, 1.0)
    cell_tags = draw_cell_tags(jax.random.fold_in(streams_of[15], 71), 0)
    fibre_ids = set_ends(jax.random.randint(streams_of[3], (NX, NY, NZ), 0, REGIONS), jax.random.fold_in(streams_of[3], 1), 0, REGIONS - 1).astype(jnp.int32)
    loan_states = jnp.clip(1.0 * jax.random.uniform(streams_of[4], (N_DEPTH * N_ROWS * N_COLS, N_COLS, CAP, STATES, CZ), jnp.float32) ** shard_levels(streams_of[4], (N_DEPTH * N_ROWS * N_COLS, N_COLS, CAP, STATES, CZ), ((0, 512),), -0.2, 0.2), 0.0, 1.0)
    loan_tags = draw_loan_tags(jax.random.fold_in(streams_of[15], 71), 0)
    lend_block = draw_lend_block(jax.random.fold_in(streams_of[15], 71), 0)
    lend_count = draw_lend_count(jax.random.fold_in(streams_of[15], 71), 0)
    diffuse_main = jnp.clip(jnp.exp(jax.random.uniform(streams_of[8], (3, REGIONS), jnp.float32, math.log(0.02), math.log(0.08))), 0.02, 0.08)
    diffuse_cross = jnp.clip(jax.random.uniform(streams_of[9], (3, REGIONS), jnp.float32, -0.02, 0.02), -0.02, 0.02)
    gate_half = jnp.clip(jax.random.uniform(streams_of[10], (3, STATES), jnp.float32, -1.0, 1.0), -1.0, 1.0)
    gate_slope = jnp.clip(jnp.exp(jax.random.uniform(streams_of[11], (3, STATES), jnp.float32, math.log(0.2), math.log(1.0))), 0.2, 1.0)
    gate_rate = jnp.clip(jnp.exp(jax.random.uniform(streams_of[12], (3, STATES), jnp.float32, math.log(0.05), math.log(3.0))), 0.05, 3.0)
    conductance = gaussian(streams_of[13], (3, STATES), STATES ** -0.5, 1.0, (), jnp.float32)
    reversal = jnp.clip(jax.random.uniform(streams_of[14], (3, STATES), jnp.float32, -1.0, 1.0), -1.0, 1.0)
    return dict(voltage=voltage, states=states, cell_tags=cell_tags, fibre_ids=fibre_ids, loan_states=loan_states, loan_tags=loan_tags, lend_block=lend_block, lend_count=lend_count, diffuse_main=diffuse_main, diffuse_cross=diffuse_cross, gate_half=gate_half, gate_slope=gate_slope, gate_rate=gate_rate, conductance=conductance, reversal=reversal)


def select_rows(table, kinds):
    marks = kinds[..., None, :]
    return jnp.where(marks == 0, table[0][:, None], jnp.where(marks == 1, table[1][:, None], table[2][:, None]))


def react(gates, potential, kinds, gate_half, gate_slope, gate_rate, conductance, reversal):
    level = potential[..., None, :]
    scaled = (level - select_rows(gate_half, kinds)) / select_rows(gate_slope, kinds)
    steady = jax.nn.sigmoid(scaled)
    decay = jnp.exp(-select_rows(gate_rate, kinds) * (1.0 + 0.5 * jnp.tanh(scaled)))
    count = jnp.where(kinds == 0, STATES, jnp.where(kinds == 1, ATRIAL, SCAR))[..., None, :]
    number = lax.broadcasted_iota(jnp.int32, gates.shape, gates.ndim - 2)
    fresh = jnp.where(number < count, steady + (gates - steady) * decay, jnp.float32(0.0))
    current = jnp.sum(select_rows(conductance, kinds) * fresh * (level - select_rows(reversal, kinds)), axis=-2)
    return fresh, current


def stencil(padded, main_coef, cross_coef):
    def offset(shift_x, shift_y, shift_z):
        return padded[1 + shift_x:padded.shape[0] - 1 + shift_x, 1 + shift_y:padded.shape[1] - 1 + shift_y, 1 + shift_z:padded.shape[2] - 1 + shift_z]
    centre = offset(0, 0, 0)
    total = main_coef[0] * (offset(1, 0, 0) + offset(-1, 0, 0) - 2.0 * centre)
    total = total + main_coef[1] * (offset(0, 1, 0) + offset(0, -1, 0) - 2.0 * centre)
    total = total + main_coef[2] * (offset(0, 0, 1) + offset(0, 0, -1) - 2.0 * centre)
    total = total + 0.5 * cross_coef[0] * (offset(1, 1, 0) - offset(1, -1, 0) - offset(-1, 1, 0) + offset(-1, -1, 0))
    total = total + 0.5 * cross_coef[1] * (offset(1, 0, 1) - offset(1, 0, -1) - offset(-1, 0, 1) + offset(-1, 0, -1))
    total = total + 0.5 * cross_coef[2] * (offset(0, 1, 1) - offset(0, 1, -1) - offset(0, -1, 1) + offset(0, -1, -1))
    return centre + total


def region_coef(table, fibre_ids):
    onehot = (fibre_ids[None] == jnp.arange(REGIONS, dtype=jnp.int32)[:, None, None, None]).astype(jnp.float32)
    return jnp.einsum("cr,rxyz->cxyz", table, onehot, precision=lax.Precision.HIGHEST)


def swap_cols(array):
    rest = array.shape[2:]
    grouped = array.reshape((N_DEPTH, N_ROWS, N_COLS, N_COLS) + rest)
    return jnp.swapaxes(grouped, 2, 3).reshape((N_DEPTH * N_ROWS * N_COLS, N_COLS) + rest)


def reference(voltage, states, cell_tags, fibre_ids, loan_states, loan_tags, lend_block, lend_count, diffuse_main, diffuse_cross, gate_half, gate_slope, gate_rate, conductance, reversal):
    tables = (gate_half, gate_slope, gate_rate, conductance, reversal)
    main_coef = region_coef(diffuse_main, fibre_ids)
    cross_coef = region_coef(diffuse_cross, fibre_ids)
    device = jnp.arange(N_DEPTH * N_ROWS * N_COLS, dtype=jnp.int32)
    depth_idx = device // (N_ROWS * N_COLS)
    rows_idx = (device // N_COLS) % N_ROWS
    cols_idx = device % N_COLS
    alive = jnp.arange(CAP, dtype=jnp.int32)[None, None, :] < lend_count[:, :, None]
    grid_x = depth_idx[:, None, None] * CX + lend_block // CY
    grid_y = rows_idx[:, None, None] * CY + lend_block % CY
    grid_x = jnp.where(alive, grid_x, NX).astype(jnp.int32)
    line_z = (cols_idx[:, None, None, None] * CZ + jnp.arange(CZ, dtype=jnp.int32)).astype(jnp.int32)
    line_z = jnp.broadcast_to(line_z, lend_block.shape + (CZ,))
    read_x = jnp.minimum(grid_x, NX - 1)[..., None]
    for step in range(STEPS):
        diffused = stencil(jnp.pad(voltage, 1), main_coef, cross_coef)

        def home_slice(pieces):
            return react(pieces[0], pieces[1], pieces[2], *tables)

        states, current = lax.map(home_slice, (states, diffused, cell_tags))
        lent_volt = diffused[read_x, grid_y[..., None], line_z]

        def loan_slice(pieces):
            return react(pieces[0], pieces[1], pieces[2], *tables)

        loan_states, loan_current = lax.map(loan_slice, (loan_states, swap_cols(lent_volt), loan_tags))
        back = swap_cols(loan_current)
        current = current.at[grid_x[..., None], grid_y[..., None], line_z].set(back, mode="drop")
        voltage = diffused - 0.25 * current
    back_states = swap_cols(loan_states)
    state_idx = jnp.arange(STATES, dtype=jnp.int32)[:, None]
    states = states.at[grid_x[..., None, None], grid_y[..., None, None], state_idx, line_z[..., None, :]].set(back_states, mode="drop")
    return voltage, states
```

```python
import jax
import jax.numpy as jnp
from jax import lax
from jax.experimental import pallas as pl
from jax.experimental.pallas import tpu as pltpu
from jax.sharding import PartitionSpec as P

STATES = 41
ATRIAL = 21
SCAR = 5
REGIONS = 8
HALF = 8
ROWS = 168
BLOCKS = 64

EARLY = (7, 6, 3, 2, 1, 0)
LATE = (5, 4)

VMEM = pl.BlockSpec(memory_space=pltpu.VMEM)
SMEM = pl.BlockSpec(memory_space=pltpu.SMEM)


def to_heavy(m):
    return [(HALF + i, i ^ m) for i in range(HALF)]


def to_light(m):
    return [(i ^ m, HALF + i) for i in range(HALF)]


def f32(*shape):
    return jax.ShapeDtypeStruct(shape, jnp.float32)


def partner(plan_ref, m):
    return HALF + jnp.bitwise_xor(plan_ref[80], m)


def gate(state, level, half, slope, rate, weight, rest):
    bent = (level - half) * slope
    steady = 0.5 + 0.5 * jnp.tanh(bent)
    decay = jnp.exp(rate * (1.0 + 0.5 * jnp.tanh(bent + bent)))
    fresh = steady + (state - steady) * decay
    return fresh, weight * fresh * (level - rest)


def react_home(tab_ref, in_ref, level, tags, out_ref):
    first, second = tags == 0, tags == 1
    current = jnp.zeros_like(level)
    for k in range(STATES):
        table = [[tab_ref[(t * 3 + m) * STATES + k] for m in range(3)] for t in range(5)]
        if k < SCAR:
            args = [jnp.where(first, a, jnp.where(second, b, c)) for a, b, c in table]
        elif k < ATRIAL:
            args = [jnp.where(first, a, b) for a, b, c in table]
        else:
            args = [a for a, b, c in table]
        rows = [(x * STATES + k) * 16 for x in range(4)]
        state = jnp.concatenate([in_ref[r : r + 16, :] for r in rows], axis=0)
        fresh, part = gate(state, level, *args)
        if k >= SCAR:
            live = first if k >= ATRIAL else tags != 2
            fresh = jnp.where(live, fresh, 0.0)
            part = jnp.where(live, part, 0.0)
        current = current + part
        for x in range(4):
            out_ref[rows[x] : rows[x] + 16, :] = fresh[16 * x : 16 * x + 16, :]
    return current


def react_lent(tab_ref, in_refs, levels, out_refs):
    low = lax.broadcasted_iota(jnp.int32, (8, 128), 0) < 4
    tags, currents = [], []
    for ref in in_refs:
        last = ref[ROWS - 8 : ROWS, :]
        tags.append(jnp.where(low, pltpu.roll(last, 4, 0), last))
        currents.append(jnp.zeros((8, 128), jnp.float32))
    for r in range(ROWS // 8):
        k0, k1 = 2 * r, min(2 * r + 1, STATES - 1)
        models = 3 if k0 < SCAR else 2 if k0 < ATRIAL else 1
        table = [
            [
                jnp.where(low, tab_ref[(t * 3 + m) * STATES + k0], tab_ref[(t * 3 + m) * STATES + k1])
                for m in range(models)
            ]
            for t in range(5)
        ]
        for j, ref in enumerate(in_refs):
            kind = tags[j]
            if models == 3:
                args = [jnp.where(kind == 0.0, a, jnp.where(kind == 1.0, b, c)) for a, b, c in table]
            elif models == 2:
                args = [jnp.where(kind == 0.0, a, b) for a, b in table]
            else:
                args = [a for (a,) in table]
            state = ref[8 * r : 8 * r + 8, :]
            fresh, part = gate(state, levels[j], *args)
            if k1 >= SCAR:
                top0 = 2.5 if k0 < SCAR else 1.5 if k0 < ATRIAL else 0.5
                top1 = 2.5 if k1 < SCAR else 1.5 if k1 < ATRIAL else 0.5
                if 2 * r + 1 >= STATES:
                    top1 = -1.0
                live = kind < (top0 if top0 == top1 else jnp.where(low, top0, top1))
                fresh = jnp.where(live, fresh, 0.0)
                part = jnp.where(live, part, 0.0)
            currents[j] = currents[j] + part
            if out_refs is not None:
                if 2 * r + 1 >= STATES:
                    fresh = jnp.where(low, fresh, state)
                out_refs[j][8 * r : 8 * r + 8, :] = fresh
    return [c + pltpu.roll(c, 4, 0) for c in currents]


def gather_lines(plan_ref, m, line_ref, hold_ref):
    p = partner(plan_ref, m)
    for s in range(4):
        row = line_ref[pl.ds(plan_ref[p * 4 + s], 1), :]
        hold_ref[s : s + 1, :] = row
        hold_ref[4 + s : 5 + s, :] = row
    return hold_ref[...]


def put_lines(plan_ref, m, hold_ref, value, line_ref):
    hold_ref[...] = value
    p = partner(plan_ref, m)
    for s in range(4):

        @pl.when(s < plan_ref[64 + p])
        def _():
            line_ref[pl.ds(plan_ref[p * 4 + s], 1), :] = hold_ref[s : s + 1, :]


def put_states(plan_ref, m, message_ref, out_ref):
    p = partner(plan_ref, m)
    for s in range(4):

        @pl.when(s < plan_ref[64 + p])
        def _():
            block = plan_ref[p * 4 + s]
            start = (block // 16) * (STATES * 16) + block % 16
            out_ref[pl.ds(start, STATES, stride=16), :] = message_ref[pl.ds(s, STATES, stride=4), :]


def stencil(coef_ref, planes_ref, before_ref, after_ref, fibre_ref, out_ref):
    lane = lax.broadcasted_iota(jnp.int32, (18, 128), 1)
    planes, slopes, sums = [], [], []
    for x in range(6):
        plane = planes_ref[x]
        lower = jnp.where(lane == 0, before_ref[x], pltpu.roll(plane, 1, 1))
        upper = jnp.where(lane == 127, after_ref[x], pltpu.roll(plane, 127, 1))
        planes.append(plane)
        slopes.append(upper - lower)
        sums.append(upper + lower)
    for x in range(1, 5):
        fibre = fibre_ref[x - 1]

        def coef(row):
            value = jnp.full((16, 128), coef_ref[row * REGIONS])
            for r in range(1, REGIONS):
                value = jnp.where(fibre == r, coef_ref[row * REGIONS + r], value)
            return value

        here, left, right = planes[x], planes[x - 1], planes[x + 1]
        centre = here[1:17]
        twice = 2.0 * centre
        total = coef(0) * (right[1:17] + left[1:17] - twice)
        total = total + coef(1) * (here[2:18] + here[0:16] - twice)
        total = total + coef(2) * (sums[x][1:17] - twice)
        total = total + 0.5 * coef(3) * (right[2:18] - right[0:16] - left[2:18] + left[0:16])
        total = total + 0.5 * coef(4) * (slopes[x + 1][1:17] - slopes[x - 1][1:17])
        total = total + 0.5 * coef(5) * (slopes[x][2:18] - slopes[x][0:16])
        out_ref[16 * (x - 1) : 16 * x, :] = centre + total


def diffuse_kernel(plan_ref, coef_ref, planes_ref, before_ref, after_ref, fibre_ref, out_ref, *line_refs):
    stencil(coef_ref, planes_ref, before_ref, after_ref, fibre_ref, out_ref)
    for m, ref in zip(LATE, line_refs):
        p = partner(plan_ref, m)
        for s in range(4):
            ref[s : s + 1, :] = out_ref[pl.ds(plan_ref[p * 4 + s], 1), :]


def home_kernel(tab_ref, states_ref, level_ref, tags_ref, out_ref, current_ref):
    current_ref[...] = react_home(tab_ref, states_ref, level_ref[...], tags_ref[...], out_ref)


def lender_kernel(tab_ref, *refs):
    n = len(LATE)
    messages, lines, outs, hold_ref = refs[:n], refs[n : 2 * n], refs[2 * n : 3 * n], refs[3 * n]
    levels = []
    for ref in lines:
        hold_ref[0:4, :] = ref[...]
        hold_ref[4:8, :] = ref[...]
        levels.append(hold_ref[...])
    for ref, current in zip(outs, react_lent(tab_ref, messages, levels, None)):
        ref[...] = current[0:4, :]


def first_kernel(plan_ref, tab_ref, level_ref, current_ref, *refs):
    n, l = len(EARLY), len(LATE)
    messages, lent = refs[:n], refs[n : n + l]
    out_ref, fresh = refs[n + l], refs[n + l + 1 : 2 * n + l + 1]
    hold_ref, sum_ref = refs[2 * n + l + 1 :]
    sum_ref[...] = current_ref[...]
    levels = [gather_lines(plan_ref, m, level_ref, hold_ref) for m in EARLY]
    currents = react_lent(tab_ref, messages, levels, fresh)
    for m, value in zip(EARLY, currents):
        put_lines(plan_ref, m, hold_ref, value, sum_ref)
    for m, ref in zip(LATE, lent):
        hold_ref[0:4, :] = ref[...]
        put_lines(plan_ref, m, hold_ref, hold_ref[...], sum_ref)
    out_ref[...] = level_ref[...] - 0.25 * sum_ref[...]


def second_kernel(plan_ref, tab_ref, coef_ref, planes_ref, before_ref, after_ref, fibre_ref, states_ref, tags_ref, *refs):
    n = len(EARLY)
    messages = refs[:n]
    level_ref, volt_ref, out_ref = refs[n : n + 3]
    hold_ref, sum_ref = refs[n + 3 : n + 5]
    fresh = refs[n + 5 :]
    stencil(coef_ref, planes_ref, before_ref, after_ref, fibre_ref, level_ref)
    sum_ref[...] = react_home(tab_ref, states_ref, level_ref[...], tags_ref[...], out_ref)
    levels = [gather_lines(plan_ref, m, level_ref, hold_ref) for m in EARLY]
    currents = react_lent(tab_ref, messages, levels, fresh)
    for m, value, ref in zip(EARLY, currents, fresh):
        put_lines(plan_ref, m, hold_ref, value, sum_ref)
        put_states(plan_ref, m, ref, out_ref)
    volt_ref[...] = level_ref[...] - 0.25 * sum_ref[...]


def last_kernel(plan_ref, tab_ref, first_ref, second_ref, volt_in, states_in, *refs):
    l = len(LATE)
    messages, (volt_ref, out_ref, hold_ref), fresh = refs[:l], refs[l : l + 3], refs[l + 3 :]
    volt_ref[...] = volt_in[...]
    out_ref[...] = states_in[...]
    levels = [gather_lines(plan_ref, m, first_ref, hold_ref) for m in LATE]
    react_lent(tab_ref, messages, levels, fresh)
    levels = [gather_lines(plan_ref, m, second_ref, hold_ref) for m in LATE]
    currents = react_lent(tab_ref, fresh, levels, fresh)
    for m, level, value, ref in zip(LATE, levels, currents, fresh):
        put_lines(plan_ref, m, hold_ref, level - 0.25 * value, volt_ref)
        put_states(plan_ref, m, ref, out_ref)


def call(body, outs, ins, scratch=(), flops=0, **kwargs):
    size = sum(4 * v.size for v in ins) + sum(4 * v.size for v in outs)
    return pl.pallas_call(
        body,
        out_shape=tuple(outs),
        in_specs=[SMEM if v.ndim == 1 else VMEM for v in ins],
        out_specs=tuple(VMEM for _ in outs),
        scratch_shapes=[pltpu.VMEM(s, jnp.float32) for s in scratch],
        compiler_params=pltpu.CompilerParams(vmem_limit_bytes=32 * 1024 * 1024),
        cost_estimate=pl.CostEstimate(flops=flops, bytes_accessed=size, transcendentals=0),
        **kwargs,
    )(*ins)


def shift(value, axis):
    peers = lax.axis_size(axis)
    return (
        lax.ppermute(value[0], axis, [(i, i + 1) for i in range(peers - 1)]),
        lax.ppermute(value[1], axis, [(i + 1, i) for i in range(peers - 1)]),
    )


def halo(field):
    before, after = shift((field[-1:], field[:1]), "depth")
    field = jnp.concatenate([before, field, after], axis=0)
    before, after = shift((field[:, -1:], field[:, :1]), "rows")
    field = jnp.concatenate([before, field, after], axis=1)
    before, after = shift((field[:, :, 127], field[:, :, 0]), "cols")
    return field, before[..., None], after[..., None]


def tied(value, *others):
    return lax.optimization_barrier((value, *others))[0]


def local(
    voltage,
    states,
    cell_tags,
    fibre_ids,
    loan_states,
    loan_tags,
    lend_block,
    lend_count,
    diffuse_main,
    diffuse_cross,
    gate_half,
    gate_slope,
    gate_rate,
    conductance,
    reversal,
):
    line = (BLOCKS, 128)
    own = lax.axis_index("cols") % HALF
    plan = jnp.concatenate([lend_block.reshape(-1), lend_count.reshape(-1), own[None].astype(jnp.int32)])
    table = jnp.concatenate(
        [t.reshape(-1) for t in (gate_half, 0.5 / gate_slope, -gate_rate, conductance, reversal)]
    )
    coef = jnp.concatenate([diffuse_main.reshape(-1), diffuse_cross.reshape(-1)])
    home = states.transpose(0, 2, 1, 3).reshape(4 * STATES * 16, 128)
    tags = cell_tags.reshape(line)

    held = loan_states[0].transpose(0, 2, 1, 3)
    held_tags = loan_tags[0].astype(jnp.float32)
    message = {}
    for m in EARLY + LATE:
        source = jnp.bitwise_xor(own, m)
        body = lax.dynamic_index_in_dim(held, source, 0, keepdims=False).reshape(STATES * 4, 128)
        kinds = lax.dynamic_index_in_dim(held_tags, source, 0, keepdims=False)
        message[m] = jnp.concatenate([body, kinds], axis=0)

    got = {}
    for m in EARLY[:3]:
        got[m] = lax.ppermute(message[m], "cols", to_heavy(m))
    diffused, *lines = call(
        diffuse_kernel,
        [f32(*line)] + [f32(4, 128) for _ in LATE],
        [plan, coef, *halo(voltage), fibre_ids],
    )
    lines = [lax.ppermute(v, "cols", to_light(m)) for m, v in zip(LATE, lines)]
    for m in EARLY[3:]:
        got[m] = lax.ppermute(tied(message[m], diffused), "cols", to_heavy(m))
    first, current = call(home_kernel, [f32(*home.shape), f32(*line)], [table, home, diffused, tags])
    back = call(
        lender_kernel,
        [f32(4, 128) for _ in LATE],
        [table, *(message[m] for m in LATE), *lines],
        scratch=[(8, 128)],
    )
    back = [lax.ppermute(v, "cols", to_heavy(m)) for m, v in zip(LATE, back)]
    for m in LATE:
        got[m] = lax.ppermute(tied(message[m], got[EARLY[3]], *back), "cols", to_heavy(m))
    volt, *fresh = call(
        first_kernel,
        [f32(*line)] + [f32(ROWS, 128) for _ in EARLY],
        [plan, table, diffused, current, *(got[m] for m in EARLY), *back],
        scratch=[(8, 128), line],
    )
    again, volt, out = call(
        second_kernel,
        [f32(*line), f32(*line), f32(*home.shape)],
        [plan, table, coef, *halo(volt.reshape(4, 16, 128)), fibre_ids, first, tags, *fresh],
        scratch=[(8, 128), line] + [(ROWS, 128) for _ in EARLY],
    )
    volt, out = call(
        last_kernel,
        [f32(*line), f32(*home.shape)],
        [plan, table, diffused, again, volt, out, *(got[m] for m in LATE)],
        scratch=[(8, 128)] + [(ROWS, 128) for _ in LATE],
    )
    return volt.reshape(4, 16, 128), out.reshape(4, STATES, 16, 128).transpose(0, 2, 1, 3)


def solution(mesh):
    brick = P("depth", "rows", "cols")
    every = ("depth", "rows", "cols")
    in_specs = (
        brick,
        P("depth", "rows", None, "cols"),
        brick,
        brick,
        P(every, None, None, None, None),
        P(every, None, None, None),
        P(every, None, None),
        P(every, None),
    ) + (P(),) * 7
    out_specs = (brick, P("depth", "rows", None, "cols"))
    return jax.shard_map(local, mesh=mesh, in_specs=in_specs, out_specs=out_specs, check_vma=False)
```

```python
import jax
import jax.numpy as jnp
from jax import lax
from jax.experimental import pallas as pl
from jax.experimental.pallas import tpu as pltpu
from jax.sharding import PartitionSpec as P

STATES = 41
ATRIAL = 21
SCAR = 5
REGIONS = 8
HALF = 8
ROWS = 168
BLOCKS = 64

EARLY = (7, 3, 2, 1, 0, 6)
LATE = (5, 4)

VMEM = pl.BlockSpec(memory_space=pltpu.VMEM)
SMEM = pl.BlockSpec(memory_space=pltpu.SMEM)


def to_heavy(m):
    return [(HALF + i, i ^ m) for i in range(HALF)]


def to_light(m):
    return [(i ^ m, HALF + i) for i in range(HALF)]


def f32(*shape):
    return jax.ShapeDtypeStruct(shape, jnp.float32)


def partner(plan_ref, m):
    return HALF + jnp.bitwise_xor(plan_ref[80], m)


def gate(state, level, half, slope, rate, weight, rest):
    bent = (level - half) * slope
    steady = 0.5 + 0.5 * jnp.tanh(bent)
    decay = jnp.exp(rate * (1.0 + 0.5 * jnp.tanh(bent + bent)))
    fresh = steady + (state - steady) * decay
    return fresh, weight * fresh * (level - rest)


def react_home(tab_ref, in_ref, level, tags, out_ref):
    first, second = tags == 0, tags == 1
    current = jnp.zeros_like(level)
    for k in range(STATES):
        table = [[tab_ref[(t * 3 + m) * STATES + k] for m in range(3)] for t in range(5)]
        if k < SCAR:
            args = [jnp.where(first, a, jnp.where(second, b, c)) for a, b, c in table]
        elif k < ATRIAL:
            args = [jnp.where(first, a, b) for a, b, c in table]
        else:
            args = [a for a, b, c in table]
        rows = [(x * STATES + k) * 16 for x in range(4)]
        state = jnp.concatenate([in_ref[r : r + 16, :] for r in rows], axis=0)
        fresh, part = gate(state, level, *args)
        if k >= SCAR:
            live = first if k >= ATRIAL else tags != 2
            fresh = jnp.where(live, fresh, 0.0)
            part = jnp.where(live, part, 0.0)
        current = current + part
        for x in range(4):
            out_ref[rows[x] : rows[x] + 16, :] = fresh[16 * x : 16 * x + 16, :]
    return current


def react_lent(tab_ref, in_refs, levels, out_refs):
    low = lax.broadcasted_iota(jnp.int32, (8, 128), 0) < 4
    tags, currents = [], []
    for ref in in_refs:
        last = ref[ROWS - 8 : ROWS, :]
        tags.append(jnp.where(low, pltpu.roll(last, 4, 0), last))
        currents.append(jnp.zeros((8, 128), jnp.float32))
    for r in range(ROWS // 8):
        k0, k1 = 2 * r, min(2 * r + 1, STATES - 1)
        models = 3 if k0 < SCAR else 2 if k0 < ATRIAL else 1
        table = [
            [
                jnp.where(low, tab_ref[(t * 3 + m) * STATES + k0], tab_ref[(t * 3 + m) * STATES + k1])
                for m in range(models)
            ]
            for t in range(5)
        ]
        for j, ref in enumerate(in_refs):
            kind = tags[j]
            if models == 3:
                args = [jnp.where(kind == 0.0, a, jnp.where(kind == 1.0, b, c)) for a, b, c in table]
            elif models == 2:
                args = [jnp.where(kind == 0.0, a, b) for a, b in table]
            else:
                args = [a for (a,) in table]
            state = ref[8 * r : 8 * r + 8, :]
            fresh, part = gate(state, levels[j], *args)
            if k1 >= SCAR:
                top0 = 2.5 if k0 < SCAR else 1.5 if k0 < ATRIAL else 0.5
                top1 = 2.5 if k1 < SCAR else 1.5 if k1 < ATRIAL else 0.5
                if 2 * r + 1 >= STATES:
                    top1 = -1.0
                live = kind < (top0 if top0 == top1 else jnp.where(low, top0, top1))
                fresh = jnp.where(live, fresh, 0.0)
                part = jnp.where(live, part, 0.0)
            currents[j] = currents[j] + part
            if out_refs is not None:
                if 2 * r + 1 >= STATES:
                    fresh = jnp.where(low, fresh, state)
                out_refs[j][8 * r : 8 * r + 8, :] = fresh
    return [c + pltpu.roll(c, 4, 0) for c in currents]


def gather_lines(plan_ref, m, line_ref, hold_ref):
    p = partner(plan_ref, m)
    for s in range(4):
        row = line_ref[pl.ds(plan_ref[p * 4 + s], 1), :]
        hold_ref[s : s + 1, :] = row
        hold_ref[4 + s : 5 + s, :] = row
    return hold_ref[...]


def put_lines(plan_ref, m, hold_ref, value, line_ref):
    hold_ref[...] = value
    p = partner(plan_ref, m)
    for s in range(4):

        @pl.when(s < plan_ref[64 + p])
        def _():
            line_ref[pl.ds(plan_ref[p * 4 + s], 1), :] = hold_ref[s : s + 1, :]


def put_states(plan_ref, m, message_ref, out_ref):
    p = partner(plan_ref, m)
    for s in range(4):

        @pl.when(s < plan_ref[64 + p])
        def _():
            block = plan_ref[p * 4 + s]
            start = (block // 16) * (STATES * 16) + block % 16
            out_ref[pl.ds(start, STATES, stride=16), :] = message_ref[pl.ds(s, STATES, stride=4), :]


def stencil(coef_ref, planes_ref, before_ref, after_ref, fibre_ref, out_ref):
    lane = lax.broadcasted_iota(jnp.int32, (18, 128), 1)
    planes, slopes, sums = [], [], []
    for x in range(6):
        plane = planes_ref[x]
        lower = jnp.where(lane == 0, before_ref[x], pltpu.roll(plane, 1, 1))
        upper = jnp.where(lane == 127, after_ref[x], pltpu.roll(plane, 127, 1))
        planes.append(plane)
        slopes.append(upper - lower)
        sums.append(upper + lower)
    for x in range(1, 5):
        fibre = fibre_ref[x - 1]

        def coef(row):
            value = jnp.full((16, 128), coef_ref[row * REGIONS])
            for r in range(1, REGIONS):
                value = jnp.where(fibre == r, coef_ref[row * REGIONS + r], value)
            return value

        here, left, right = planes[x], planes[x - 1], planes[x + 1]
        centre = here[1:17]
        twice = 2.0 * centre
        total = coef(0) * (right[1:17] + left[1:17] - twice)
        total = total + coef(1) * (here[2:18] + here[0:16] - twice)
        total = total + coef(2) * (sums[x][1:17] - twice)
        total = total + 0.5 * coef(3) * (right[2:18] - right[0:16] - left[2:18] + left[0:16])
        total = total + 0.5 * coef(4) * (slopes[x + 1][1:17] - slopes[x - 1][1:17])
        total = total + 0.5 * coef(5) * (slopes[x][2:18] - slopes[x][0:16])
        out_ref[16 * (x - 1) : 16 * x, :] = centre + total


def diffuse_kernel(plan_ref, coef_ref, planes_ref, before_ref, after_ref, fibre_ref, out_ref, *line_refs):
    stencil(coef_ref, planes_ref, before_ref, after_ref, fibre_ref, out_ref)
    for m, ref in zip(LATE, line_refs):
        p = partner(plan_ref, m)
        for s in range(4):
            ref[s : s + 1, :] = out_ref[pl.ds(plan_ref[p * 4 + s], 1), :]


def home_kernel(tab_ref, states_ref, level_ref, tags_ref, out_ref, current_ref):
    current_ref[...] = react_home(tab_ref, states_ref, level_ref[...], tags_ref[...], out_ref)


def lender_kernel(tab_ref, *refs):
    n = len(LATE)
    messages, lines, outs, hold_ref = refs[:n], refs[n : 2 * n], refs[2 * n : 3 * n], refs[3 * n]
    levels = []
    for ref in lines:
        hold_ref[0:4, :] = ref[...]
        hold_ref[4:8, :] = ref[...]
        levels.append(hold_ref[...])
    for ref, current in zip(outs, react_lent(tab_ref, messages, levels, None)):
        ref[...] = current[0:4, :]


def first_kernel(plan_ref, tab_ref, level_ref, current_ref, *refs):
    n, l = len(EARLY), len(LATE)
    messages, lent = refs[:n], refs[n : n + l]
    out_ref, fresh = refs[n + l], refs[n + l + 1 : 2 * n + l + 1]
    hold_ref, sum_ref = refs[2 * n + l + 1 :]
    sum_ref[...] = current_ref[...]
    levels = [gather_lines(plan_ref, m, level_ref, hold_ref) for m in EARLY]
    currents = react_lent(tab_ref, messages, levels, fresh)
    for m, value in zip(EARLY, currents):
        put_lines(plan_ref, m, hold_ref, value, sum_ref)
    for m, ref in zip(LATE, lent):
        hold_ref[0:4, :] = ref[...]
        put_lines(plan_ref, m, hold_ref, hold_ref[...], sum_ref)
    out_ref[...] = level_ref[...] - 0.25 * sum_ref[...]


def second_kernel(plan_ref, tab_ref, coef_ref, planes_ref, before_ref, after_ref, fibre_ref, states_ref, tags_ref, *refs):
    n = len(EARLY)
    messages = refs[:n]
    level_ref, volt_ref, out_ref = refs[n : n + 3]
    hold_ref, sum_ref = refs[n + 3 : n + 5]
    fresh = refs[n + 5 :]
    stencil(coef_ref, planes_ref, before_ref, after_ref, fibre_ref, level_ref)
    sum_ref[...] = react_home(tab_ref, states_ref, level_ref[...], tags_ref[...], out_ref)
    levels = [gather_lines(plan_ref, m, level_ref, hold_ref) for m in EARLY]
    currents = react_lent(tab_ref, messages, levels, fresh)
    for m, value, ref in zip(EARLY, currents, fresh):
        put_lines(plan_ref, m, hold_ref, value, sum_ref)
        put_states(plan_ref, m, ref, out_ref)
    volt_ref[...] = level_ref[...] - 0.25 * sum_ref[...]


def last_kernel(plan_ref, tab_ref, first_ref, second_ref, volt_in, states_in, *refs):
    l = len(LATE)
    messages, (volt_ref, out_ref, hold_ref), fresh = refs[:l], refs[l : l + 3], refs[l + 3 :]
    volt_ref[...] = volt_in[...]
    out_ref[...] = states_in[...]
    levels = [gather_lines(plan_ref, m, first_ref, hold_ref) for m in LATE]
    react_lent(tab_ref, messages, levels, fresh)
    levels = [gather_lines(plan_ref, m, second_ref, hold_ref) for m in LATE]
    currents = react_lent(tab_ref, fresh, levels, fresh)
    for m, level, value, ref in zip(LATE, levels, currents, fresh):
        put_lines(plan_ref, m, hold_ref, level - 0.25 * value, volt_ref)
        put_states(plan_ref, m, ref, out_ref)


def call(body, outs, ins, scratch=(), flops=0, **kwargs):
    size = sum(4 * v.size for v in ins) + sum(4 * v.size for v in outs)
    return pl.pallas_call(
        body,
        out_shape=tuple(outs),
        in_specs=[SMEM if v.ndim == 1 else VMEM for v in ins],
        out_specs=tuple(VMEM for _ in outs),
        scratch_shapes=[pltpu.VMEM(s, jnp.float32) for s in scratch],
        compiler_params=pltpu.CompilerParams(vmem_limit_bytes=32 * 1024 * 1024),
        cost_estimate=pl.CostEstimate(flops=flops, bytes_accessed=size, transcendentals=0),
        **kwargs,
    )(*ins)


def shift(value, axis):
    peers = lax.axis_size(axis)
    return (
        lax.ppermute(value[0], axis, [(i, i + 1) for i in range(peers - 1)]),
        lax.ppermute(value[1], axis, [(i + 1, i) for i in range(peers - 1)]),
    )


def beside_depth(field):
    place, peers = lax.axis_index("depth"), lax.axis_size("depth")
    layers = lax.all_gather(jnp.concatenate([field[:1], field[-1:]], axis=0), "depth")
    lower = lax.dynamic_index_in_dim(layers, jnp.maximum(place - 1, 0), 0, keepdims=False)
    upper = lax.dynamic_index_in_dim(layers, jnp.minimum(place + 1, peers - 1), 0, keepdims=False)
    return jnp.where(place > 0, lower[1:], 0.0), jnp.where(place < peers - 1, upper[:1], 0.0)


def halo(field, send=lambda phase, *after: ()):
    field = tied(field, *send("depth", field))
    before, after = beside_depth(field)
    field = jnp.concatenate([before, field, after], axis=0)
    field = tied(field, *send("rows", field))
    before, after = shift((field[:, -1:], field[:, :1]), "rows")
    field = jnp.concatenate([before, field, after], axis=1)
    field = tied(field, *send("cols", field))
    before, after = shift((field[:, :, 127], field[:, :, 0]), "cols")
    return field, before[..., None], after[..., None]


def tied(value, *others):
    if not others:
        return value
    return lax.optimization_barrier((value, *others))[0]


def local(
    voltage,
    states,
    cell_tags,
    fibre_ids,
    loan_states,
    loan_tags,
    lend_block,
    lend_count,
    diffuse_main,
    diffuse_cross,
    gate_half,
    gate_slope,
    gate_rate,
    conductance,
    reversal,
):
    line = (BLOCKS, 128)
    own = lax.axis_index("cols") % HALF
    plan = jnp.concatenate([lend_block.reshape(-1), lend_count.reshape(-1), own[None].astype(jnp.int32)])
    table = jnp.concatenate(
        [t.reshape(-1) for t in (gate_half, 0.5 / gate_slope, -gate_rate, conductance, reversal)]
    )
    coef = jnp.concatenate([diffuse_main.reshape(-1), diffuse_cross.reshape(-1)])
    home = states.transpose(0, 2, 1, 3).reshape(4 * STATES * 16, 128)
    tags = cell_tags.reshape(line)

    held = loan_states[0].transpose(0, 2, 1, 3)
    message = {}
    for m in EARLY + LATE:
        source = jnp.bitwise_xor(own, m)
        body = lax.dynamic_index_in_dim(held, source, 0, keepdims=False).reshape(STATES * 4, 128)
        kinds = lax.dynamic_index_in_dim(loan_tags[0], source, 0, keepdims=False)
        message[m] = jnp.concatenate([body, kinds.astype(jnp.float32)], axis=0)

    got = {}

    def send(m, *after):
        got[m] = lax.ppermute(tied(message[m], *after), "cols", to_heavy(m))

    e0, e1, e2, e3, e4, e5 = EARLY
    send(e0)
    send(e1)
    send(e2)

    def beside(phase, field):
        if phase == "depth":
            return message[e0], message[e1], message[e2]
        if phase == "cols":
            send(e3, field, got[e0])
            return (got[e0],)
        return ()

    diffused, *lines = call(
        diffuse_kernel,
        [f32(*line)] + [f32(4, 128) for _ in LATE],
        [plan, coef, *halo(voltage, beside), fibre_ids],
    )
    send(e4, diffused, got[e1])
    send(e5, diffused, got[e2])
    lines = [lax.ppermute(tied(v, got[e1], got[e2]), "cols", to_light(m)) for m, v in zip(LATE, lines)]
    first, current = call(home_kernel, [f32(*home.shape), f32(*line)], [table, home, diffused, tags])
    back = call(
        lender_kernel,
        [f32(4, 128) for _ in LATE],
        [table, *(message[m] for m in LATE), *(tied(v, current, got[e3]) for v in lines)],
        scratch=[(8, 128)],
    )
    back = [lax.ppermute(v, "cols", to_heavy(m)) for m, v in zip(LATE, back)]
    volt, *fresh = call(
        first_kernel,
        [f32(*line)] + [f32(ROWS, 128) for _ in EARLY],
        [plan, table, diffused, current, *(got[m] for m in EARLY), *back],
        scratch=[(8, 128), line],
    )

    def beside_second(phase, field):
        if phase == "depth":
            send(LATE[0], field)
        elif phase == "rows":
            send(LATE[1], field)
        return ()

    again, volt, out = call(
        second_kernel,
        [f32(*line), f32(*line), f32(*home.shape)],
        [plan, table, coef, *halo(volt.reshape(4, 16, 128), beside_second), fibre_ids, first, tags, *fresh],
        scratch=[(8, 128), line] + [(ROWS, 128) for _ in EARLY],
    )
    volt, out = call(
        last_kernel,
        [f32(*line), f32(*home.shape)],
        [plan, table, diffused, again, volt, out, *(got[m] for m in LATE)],
        scratch=[(8, 128)] + [(ROWS, 128) for _ in LATE],
    )
    return volt.reshape(4, 16, 128), out.reshape(4, STATES, 16, 128).transpose(0, 2, 1, 3)


def solution(mesh):
    brick = P("depth", "rows", "cols")
    every = ("depth", "rows", "cols")
    in_specs = (
        brick,
        P("depth", "rows", None, "cols"),
        brick,
        brick,
        P(every, None, None, None, None),
        P(every, None, None, None),
        P(every, None, None),
        P(every, None),
    ) + (P(),) * 7
    out_specs = (brick, P("depth", "rows", None, "cols"))
    return jax.shard_map(local, mesh=mesh, in_specs=in_specs, out_specs=out_specs, check_vma=False)
```

```python
import jax
import jax.numpy as jnp
from jax import lax
from jax.experimental import pallas as pl
from jax.experimental.pallas import tpu as pltpu
from jax.sharding import PartitionSpec as P

STATES = 41
ATRIAL = 21
SCAR = 5
REGIONS = 8
HALF = 8
ROWS = 168
BLOCKS = 64

EARLY = (7, 3, 2, 1, 0, 6)
SOON = 4
LATE = (5, 4)

VMEM = pl.BlockSpec(memory_space=pltpu.VMEM)
SMEM = pl.BlockSpec(memory_space=pltpu.SMEM)


def to_heavy(m):
    return [(HALF + i, i ^ m) for i in range(HALF)]


def to_light(m):
    return [(i ^ m, HALF + i) for i in range(HALF)]


def f32(*shape):
    return jax.ShapeDtypeStruct(shape, jnp.float32)


def partner(plan_ref, m):
    return HALF + jnp.bitwise_xor(plan_ref[80], m)


def gate(state, level, half, slope, rate, weight, rest):
    bent = (level - half) * slope
    steady = 0.5 + 0.5 * jnp.tanh(bent)
    decay = jnp.exp(rate * (1.0 + 0.5 * jnp.tanh(bent + bent)))
    fresh = steady + (state - steady) * decay
    return fresh, weight * fresh * (level - rest)


def react_home(tab_ref, in_ref, level, tags, out_ref):
    first, second = tags == 0, tags == 1
    current = jnp.zeros_like(level)
    for k in range(STATES):
        table = [[tab_ref[(t * 3 + m) * STATES + k] for m in range(3)] for t in range(5)]
        if k < SCAR:
            args = [jnp.where(first, a, jnp.where(second, b, c)) for a, b, c in table]
        elif k < ATRIAL:
            args = [jnp.where(first, a, b) for a, b, c in table]
        else:
            args = [a for a, b, c in table]
        rows = [(x * STATES + k) * 16 for x in range(4)]
        state = jnp.concatenate([in_ref[r : r + 16, :] for r in rows], axis=0)
        fresh, part = gate(state, level, *args)
        if k >= SCAR:
            live = first if k >= ATRIAL else tags != 2
            fresh = jnp.where(live, fresh, 0.0)
            part = jnp.where(live, part, 0.0)
        current = current + part
        for x in range(4):
            out_ref[rows[x] : rows[x] + 16, :] = fresh[16 * x : 16 * x + 16, :]
    return current


def react_lent(tab_ref, in_refs, levels, out_refs):
    low = lax.broadcasted_iota(jnp.int32, (8, 128), 0) < 4
    tags, currents = [], []
    for ref in in_refs:
        last = ref[ROWS - 8 : ROWS, :]
        tags.append(jnp.where(low, pltpu.roll(last, 4, 0), last))
        currents.append(jnp.zeros((8, 128), jnp.float32))
    for r in range(ROWS // 8):
        k0, k1 = 2 * r, min(2 * r + 1, STATES - 1)
        models = 3 if k0 < SCAR else 2 if k0 < ATRIAL else 1
        table = [
            [
                jnp.where(low, tab_ref[(t * 3 + m) * STATES + k0], tab_ref[(t * 3 + m) * STATES + k1])
                for m in range(models)
            ]
            for t in range(5)
        ]
        for j, ref in enumerate(in_refs):
            kind = tags[j]
            if models == 3:
                args = [jnp.where(kind == 0.0, a, jnp.where(kind == 1.0, b, c)) for a, b, c in table]
            elif models == 2:
                args = [jnp.where(kind == 0.0, a, b) for a, b in table]
            else:
                args = [a for (a,) in table]
            state = ref[8 * r : 8 * r + 8, :]
            fresh, part = gate(state, levels[j], *args)
            if k1 >= SCAR:
                top0 = 2.5 if k0 < SCAR else 1.5 if k0 < ATRIAL else 0.5
                top1 = 2.5 if k1 < SCAR else 1.5 if k1 < ATRIAL else 0.5
                if 2 * r + 1 >= STATES:
                    top1 = -1.0
                live = kind < (top0 if top0 == top1 else jnp.where(low, top0, top1))
                fresh = jnp.where(live, fresh, 0.0)
                part = jnp.where(live, part, 0.0)
            currents[j] = currents[j] + part
            if out_refs is not None:
                if 2 * r + 1 >= STATES:
                    fresh = jnp.where(low, fresh, state)
                out_refs[j][8 * r : 8 * r + 8, :] = fresh
    return [c + pltpu.roll(c, 4, 0) for c in currents]


def gather_lines(plan_ref, m, line_ref, hold_ref):
    p = partner(plan_ref, m)
    for s in range(4):
        row = line_ref[pl.ds(plan_ref[p * 4 + s], 1), :]
        hold_ref[s : s + 1, :] = row
        hold_ref[4 + s : 5 + s, :] = row
    return hold_ref[...]


def put_lines(plan_ref, m, hold_ref, value, line_ref):
    hold_ref[...] = value
    p = partner(plan_ref, m)
    for s in range(4):

        @pl.when(s < plan_ref[64 + p])
        def _():
            line_ref[pl.ds(plan_ref[p * 4 + s], 1), :] = hold_ref[s : s + 1, :]


def put_states(plan_ref, m, message_ref, out_ref):
    p = partner(plan_ref, m)
    for s in range(4):

        @pl.when(s < plan_ref[64 + p])
        def _():
            block = plan_ref[p * 4 + s]
            start = (block // 16) * (STATES * 16) + block % 16
            out_ref[pl.ds(start, STATES, stride=16), :] = message_ref[pl.ds(s, STATES, stride=4), :]


def stencil(coef_ref, planes_ref, before_ref, after_ref, fibre_ref, out_ref):
    lane = lax.broadcasted_iota(jnp.int32, (18, 128), 1)
    planes, slopes, sums = [], [], []
    for x in range(6):
        plane = planes_ref[x]
        lower = jnp.where(lane == 0, before_ref[x], pltpu.roll(plane, 1, 1))
        upper = jnp.where(lane == 127, after_ref[x], pltpu.roll(plane, 127, 1))
        planes.append(plane)
        slopes.append(upper - lower)
        sums.append(upper + lower)
    for x in range(1, 5):
        fibre = fibre_ref[x - 1]

        def coef(row):
            value = jnp.full((16, 128), coef_ref[row * REGIONS])
            for r in range(1, REGIONS):
                value = jnp.where(fibre == r, coef_ref[row * REGIONS + r], value)
            return value

        here, left, right = planes[x], planes[x - 1], planes[x + 1]
        centre = here[1:17]
        twice = 2.0 * centre
        total = coef(0) * (right[1:17] + left[1:17] - twice)
        total = total + coef(1) * (here[2:18] + here[0:16] - twice)
        total = total + coef(2) * (sums[x][1:17] - twice)
        total = total + 0.5 * coef(3) * (right[2:18] - right[0:16] - left[2:18] + left[0:16])
        total = total + 0.5 * coef(4) * (slopes[x + 1][1:17] - slopes[x - 1][1:17])
        total = total + 0.5 * coef(5) * (slopes[x][2:18] - slopes[x][0:16])
        out_ref[16 * (x - 1) : 16 * x, :] = centre + total


def diffuse_kernel(plan_ref, coef_ref, planes_ref, before_ref, after_ref, fibre_ref, out_ref, *line_refs):
    stencil(coef_ref, planes_ref, before_ref, after_ref, fibre_ref, out_ref)
    for m, ref in zip(LATE, line_refs):
        p = partner(plan_ref, m)
        for s in range(4):
            ref[s : s + 1, :] = out_ref[pl.ds(plan_ref[p * 4 + s], 1), :]


def home_kernel(tab_ref, states_ref, level_ref, tags_ref, out_ref, current_ref):
    current_ref[...] = react_home(tab_ref, states_ref, level_ref[...], tags_ref[...], out_ref)


def lender_kernel(tab_ref, *refs):
    n = len(LATE)
    messages, lines, outs, hold_ref = refs[:n], refs[n : 2 * n], refs[2 * n : 3 * n], refs[3 * n]
    levels = []
    for ref in lines:
        hold_ref[0:4, :] = ref[...]
        hold_ref[4:8, :] = ref[...]
        levels.append(hold_ref[...])
    for ref, current in zip(outs, react_lent(tab_ref, messages, levels, None)):
        ref[...] = current[0:4, :]


def early_kernel(plan_ref, tab_ref, level_ref, current_ref, *refs):
    messages, out_ref, fresh, hold_ref = refs[:SOON], refs[SOON], refs[SOON + 1 : 2 * SOON + 1], refs[-1]
    out_ref[...] = current_ref[...]
    levels = [gather_lines(plan_ref, m, level_ref, hold_ref) for m in EARLY[:SOON]]
    currents = react_lent(tab_ref, messages, levels, fresh)
    for m, value in zip(EARLY[:SOON], currents):
        put_lines(plan_ref, m, hold_ref, value, out_ref)


def first_kernel(plan_ref, tab_ref, level_ref, current_ref, *refs):
    rest = EARLY[SOON:]
    n, l = len(rest), len(LATE)
    messages, lent = refs[:n], refs[n : n + l]
    out_ref, fresh = refs[n + l], refs[n + l + 1 : 2 * n + l + 1]
    hold_ref, sum_ref = refs[2 * n + l + 1 :]
    sum_ref[...] = current_ref[...]
    levels = [gather_lines(plan_ref, m, level_ref, hold_ref) for m in rest]
    currents = react_lent(tab_ref, messages, levels, fresh)
    for m, value in zip(rest, currents):
        put_lines(plan_ref, m, hold_ref, value, sum_ref)
    for m, ref in zip(LATE, lent):
        hold_ref[0:4, :] = ref[...]
        put_lines(plan_ref, m, hold_ref, hold_ref[...], sum_ref)
    out_ref[...] = level_ref[...] - 0.25 * sum_ref[...]


def second_kernel(plan_ref, tab_ref, coef_ref, planes_ref, before_ref, after_ref, fibre_ref, first_ref, states_ref, tags_ref, *refs):
    n, l = len(EARLY), len(LATE)
    early, late = refs[:n], refs[n : n + l]
    volt_ref, out_ref, hold_ref, level_ref, sum_ref = refs[n + l : n + l + 5]
    fresh = refs[n + l + 5 :]
    levels = [gather_lines(plan_ref, m, first_ref, hold_ref) for m in LATE]
    react_lent(tab_ref, late, levels, fresh[n:])
    stencil(coef_ref, planes_ref, before_ref, after_ref, fibre_ref, level_ref)
    sum_ref[...] = react_home(tab_ref, states_ref, level_ref[...], tags_ref[...], out_ref)
    levels = [gather_lines(plan_ref, m, level_ref, hold_ref) for m in EARLY + LATE]
    currents = react_lent(tab_ref, (*early, *fresh[n:]), levels, fresh)
    for m, value, ref in zip(EARLY + LATE, currents, fresh):
        put_lines(plan_ref, m, hold_ref, value, sum_ref)
        put_states(plan_ref, m, ref, out_ref)
    volt_ref[...] = level_ref[...] - 0.25 * sum_ref[...]


def call(body, outs, ins, scratch=(), flops=0, **kwargs):
    size = sum(4 * v.size for v in ins) + sum(4 * v.size for v in outs)
    return pl.pallas_call(
        body,
        out_shape=tuple(outs),
        in_specs=[SMEM if v.ndim == 1 else VMEM for v in ins],
        out_specs=tuple(VMEM for _ in outs),
        scratch_shapes=[pltpu.VMEM(s, jnp.float32) for s in scratch],
        compiler_params=pltpu.CompilerParams(vmem_limit_bytes=32 * 1024 * 1024),
        cost_estimate=pl.CostEstimate(flops=flops, bytes_accessed=size, transcendentals=0),
        **kwargs,
    )(*ins)


def shift(value, axis):
    peers = lax.axis_size(axis)
    return (
        lax.ppermute(value[0], axis, [(i, i + 1) for i in range(peers - 1)]),
        lax.ppermute(value[1], axis, [(i + 1, i) for i in range(peers - 1)]),
    )


def beside_depth(field):
    place, peers = lax.axis_index("depth"), lax.axis_size("depth")
    layers = lax.all_gather(jnp.concatenate([field[:1], field[-1:]], axis=0), "depth")
    lower = lax.dynamic_index_in_dim(layers, jnp.maximum(place - 1, 0), 0, keepdims=False)
    upper = lax.dynamic_index_in_dim(layers, jnp.minimum(place + 1, peers - 1), 0, keepdims=False)
    return jnp.where(place > 0, lower[1:], 0.0), jnp.where(place < peers - 1, upper[:1], 0.0)


def halo_depth_last(field, send):
    send("rows", field)
    before, after = shift((field[:, -1:], field[:, :1]), "rows")
    field = jnp.concatenate([before, field, after], axis=1)
    before, after = shift((field[:, :, 127], field[:, :, 0]), "cols")
    count = field.shape[1]

    def face(x):
        columns = jnp.pad(jnp.stack([before[x], after[x]]), ((0, 4), (0, 128 - count)))
        return jnp.concatenate([field[x], columns], axis=0)

    place, peers = lax.axis_index("depth"), lax.axis_size("depth")
    layers = lax.all_gather(jnp.stack([face(0), face(-1)]), "depth")
    lower = lax.dynamic_index_in_dim(layers, jnp.maximum(place - 1, 0), 0, keepdims=False)[1:]
    upper = lax.dynamic_index_in_dim(layers, jnp.minimum(place + 1, peers - 1), 0, keepdims=False)[:1]
    lower, upper = jnp.where(place > 0, lower, 0.0), jnp.where(place < peers - 1, upper, 0.0)
    field = jnp.concatenate([lower[:, :count], field, upper[:, :count]], axis=0)
    before = jnp.concatenate([lower[:, count, :count], before, upper[:, count, :count]], axis=0)
    after = jnp.concatenate([lower[:, count + 1, :count], after, upper[:, count + 1, :count]], axis=0)
    return field, before[..., None], after[..., None]


def halo(field, send=lambda phase, *after: ()):
    field = tied(field, *send("depth", field))
    before, after = beside_depth(field)
    field = jnp.concatenate([before, field, after], axis=0)
    field = tied(field, *send("rows", field))
    before, after = shift((field[:, -1:], field[:, :1]), "rows")
    field = jnp.concatenate([before, field, after], axis=1)
    field = tied(field, *send("cols", field))
    before, after = shift((field[:, :, 127], field[:, :, 0]), "cols")
    return field, before[..., None], after[..., None]


def tied(value, *others):
    if not others:
        return value
    return lax.optimization_barrier((value, *others))[0]


def local(
    voltage,
    states,
    cell_tags,
    fibre_ids,
    loan_states,
    loan_tags,
    lend_block,
    lend_count,
    diffuse_main,
    diffuse_cross,
    gate_half,
    gate_slope,
    gate_rate,
    conductance,
    reversal,
):
    line = (BLOCKS, 128)
    own = lax.axis_index("cols") % HALF
    plan = jnp.concatenate([lend_block.reshape(-1), lend_count.reshape(-1), own[None].astype(jnp.int32)])
    table = jnp.concatenate(
        [t.reshape(-1) for t in (gate_half, 0.5 / gate_slope, -gate_rate, conductance, reversal)]
    )
    coef = jnp.concatenate([diffuse_main.reshape(-1), diffuse_cross.reshape(-1)])
    home = states.transpose(0, 2, 1, 3).reshape(4 * STATES * 16, 128)
    tags = cell_tags.reshape(line)

    held = loan_states[0].transpose(0, 2, 1, 3)
    message = {}
    for m in EARLY + LATE:
        source = jnp.bitwise_xor(own, m)
        body = lax.dynamic_index_in_dim(held, source, 0, keepdims=False).reshape(STATES * 4, 128)
        kinds = lax.dynamic_index_in_dim(loan_tags[0], source, 0, keepdims=False)
        message[m] = jnp.concatenate([body, kinds.astype(jnp.float32)], axis=0)

    got = {}

    def send(m, *after):
        got[m] = lax.ppermute(tied(message[m], *after), "cols", to_heavy(m))

    e0, e1, e2, e3, e4, e5 = EARLY
    send(e0)
    send(e1)
    send(e2)

    def beside(phase, field):
        if phase == "depth":
            return message[e0], message[e1], message[e2]
        if phase == "cols":
            send(e3, field, got[e0])
            return (got[e0],)
        return ()

    diffused, *lines = call(
        diffuse_kernel,
        [f32(*line)] + [f32(4, 128) for _ in LATE],
        [plan, coef, *halo(voltage, beside), fibre_ids],
    )
    send(e4, diffused, got[e1])
    send(e5, diffused, got[e2])
    lines = [lax.ppermute(tied(v, got[e1], got[e2]), "cols", to_light(m)) for m, v in zip(LATE, lines)]
    back = call(
        lender_kernel,
        [f32(4, 128) for _ in LATE],
        [table, *(message[m] for m in LATE), *lines],
        scratch=[(8, 128)],
    )
    first, current = call(
        home_kernel, [f32(*home.shape), f32(*line)], [table, home, tied(diffused, *back), tags]
    )
    back = [lax.ppermute(v, "cols", to_heavy(m)) for m, v in zip(LATE, back)]
    current, *fresh = call(
        early_kernel,
        [f32(*line)] + [f32(ROWS, 128) for _ in EARLY[:SOON]],
        [plan, table, diffused, current, *(got[m] for m in EARLY[:SOON])],
        scratch=[(8, 128)],
    )
    volt, *others = call(
        first_kernel,
        [f32(*line)] + [f32(ROWS, 128) for _ in EARLY[SOON:]],
        [plan, table, diffused, current, *(got[m] for m in EARLY[SOON:]), *back],
        scratch=[(8, 128), line],
    )
    fresh += others

    def beside_second(phase, field):
        for m in LATE:
            send(m, field)

    planes = halo_depth_last(volt.reshape(4, 16, 128), beside_second)
    late = [got[m] for m in LATE]
    volt, out = call(
        second_kernel,
        [f32(*line), f32(*home.shape)],
        [plan, table, coef, *planes, fibre_ids, diffused, first, tags, *fresh, *late],
        scratch=[(8, 128), line, line] + [(ROWS, 128) for _ in EARLY + LATE],
    )
    return volt.reshape(4, 16, 128), out.reshape(4, STATES, 16, 128).transpose(0, 2, 1, 3)


def solution(mesh):
    brick = P("depth", "rows", "cols")
    every = ("depth", "rows", "cols")
    in_specs = (
        brick,
        P("depth", "rows", None, "cols"),
        brick,
        brick,
        P(every, None, None, None, None),
        P(every, None, None, None),
        P(every, None, None),
        P(every, None),
    ) + (P(),) * 7
    out_specs = (brick, P("depth", "rows", None, "cols"))
    return jax.shard_map(local, mesh=mesh, in_specs=in_specs, out_specs=out_specs, check_vma=False)
```

```python
import jax
import jax.numpy as jnp
from jax import lax
from jax.experimental import pallas as pl
from jax.experimental.pallas import tpu as pltpu
from jax.sharding import PartitionSpec as P

STATES = 41
ATRIAL = 21
SCAR = 5
REGIONS = 8
HALF = 8
ROWS = 168
BLOCKS = 64

EARLY = (7, 3, 2, 1, 0, 6)
SOON = 4
LATE = (5, 4)

VMEM = pl.BlockSpec(memory_space=pltpu.VMEM)
SMEM = pl.BlockSpec(memory_space=pltpu.SMEM)


def to_heavy(m):
    return [(HALF + i, i ^ m) for i in range(HALF)]


def to_light(m):
    return [(i ^ m, HALF + i) for i in range(HALF)]


def f32(*shape):
    return jax.ShapeDtypeStruct(shape, jnp.float32)


def partner(plan_ref, m):
    return HALF + jnp.bitwise_xor(plan_ref[80], m)


def gate(state, level, half, slope, rate, weight, rest):
    bent = (level - half) * slope
    steady = 0.5 + 0.5 * jnp.tanh(bent)
    decay = jnp.exp(rate * (1.0 + 0.5 * jnp.tanh(bent + bent)))
    fresh = steady + (state - steady) * decay
    return fresh, weight * fresh * (level - rest)


def react_home(tab_ref, in_ref, level, tags, out_ref):
    first, second = tags == 0, tags == 1
    current = jnp.zeros_like(level)
    for k in range(STATES):
        table = [[tab_ref[(t * 3 + m) * STATES + k] for m in range(3)] for t in range(5)]
        if k < SCAR:
            args = [jnp.where(first, a, jnp.where(second, b, c)) for a, b, c in table]
        elif k < ATRIAL:
            args = [jnp.where(first, a, b) for a, b, c in table]
        else:
            args = [a for a, b, c in table]
        rows = [(x * STATES + k) * 16 for x in range(4)]
        state = jnp.concatenate([in_ref[r : r + 16, :] for r in rows], axis=0)
        fresh, part = gate(state, level, *args)
        if k >= SCAR:
            live = first if k >= ATRIAL else tags != 2
            fresh = jnp.where(live, fresh, 0.0)
            part = jnp.where(live, part, 0.0)
        current = current + part
        for x in range(4):
            out_ref[rows[x] : rows[x] + 16, :] = fresh[16 * x : 16 * x + 16, :]
    return current


def react_lent(tab_ref, in_refs, levels, out_refs):
    low = lax.broadcasted_iota(jnp.int32, (8, 128), 0) < 4
    tags, currents = [], []
    for ref in in_refs:
        last = ref[ROWS - 8 : ROWS, :]
        tags.append(jnp.where(low, pltpu.roll(last, 4, 0), last))
        currents.append(jnp.zeros((8, 128), jnp.float32))
    for r in range(ROWS // 8):
        k0, k1 = 2 * r, min(2 * r + 1, STATES - 1)
        models = 3 if k0 < SCAR else 2 if k0 < ATRIAL else 1
        table = [
            [
                jnp.where(low, tab_ref[(t * 3 + m) * STATES + k0], tab_ref[(t * 3 + m) * STATES + k1])
                for m in range(models)
            ]
            for t in range(5)
        ]
        for j, ref in enumerate(in_refs):
            kind = tags[j]
            if models == 3:
                args = [jnp.where(kind == 0.0, a, jnp.where(kind == 1.0, b, c)) for a, b, c in table]
            elif models == 2:
                args = [jnp.where(kind == 0.0, a, b) for a, b in table]
            else:
                args = [a for (a,) in table]
            state = ref[8 * r : 8 * r + 8, :]
            fresh, part = gate(state, levels[j], *args)
            if k1 >= SCAR:
                top0 = 2.5 if k0 < SCAR else 1.5 if k0 < ATRIAL else 0.5
                top1 = 2.5 if k1 < SCAR else 1.5 if k1 < ATRIAL else 0.5
                if 2 * r + 1 >= STATES:
                    top1 = -1.0
                live = kind < (top0 if top0 == top1 else jnp.where(low, top0, top1))
                fresh = jnp.where(live, fresh, 0.0)
                part = jnp.where(live, part, 0.0)
            currents[j] = currents[j] + part
            if out_refs is not None:
                if 2 * r + 1 >= STATES:
                    fresh = jnp.where(low, fresh, state)
                out_refs[j][8 * r : 8 * r + 8, :] = fresh
    return [c + pltpu.roll(c, 4, 0) for c in currents]


def gather_lines(plan_ref, m, line_ref, hold_ref):
    p = partner(plan_ref, m)
    for s in range(4):
        row = line_ref[pl.ds(plan_ref[p * 4 + s], 1), :]
        hold_ref[s : s + 1, :] = row
        hold_ref[4 + s : 5 + s, :] = row
    return hold_ref[...]


def put_lines(plan_ref, m, hold_ref, value, line_ref):
    hold_ref[...] = value
    p = partner(plan_ref, m)
    for s in range(4):

        @pl.when(s < plan_ref[64 + p])
        def _():
            line_ref[pl.ds(plan_ref[p * 4 + s], 1), :] = hold_ref[s : s + 1, :]


def put_states(plan_ref, m, message_ref, out_ref):
    p = partner(plan_ref, m)
    for s in range(4):

        @pl.when(s < plan_ref[64 + p])
        def _():
            block = plan_ref[p * 4 + s]
            start = (block // 16) * (STATES * 16) + block % 16
            out_ref[pl.ds(start, 40, stride=16), :] = message_ref[pl.ds(s, 40, stride=4), :]
            out_ref[pl.ds(start + 640, 1), :] = message_ref[160 + s : 161 + s, :]


def stencil(coef_ref, planes_ref, before_ref, after_ref, fibre_ref, out_ref):
    lane = lax.broadcasted_iota(jnp.int32, (18, 128), 1)
    planes, slopes, sums = [], [], []
    for x in range(6):
        plane = planes_ref[x]
        lower = jnp.where(lane == 0, before_ref[x], pltpu.roll(plane, 1, 1))
        upper = jnp.where(lane == 127, after_ref[x], pltpu.roll(plane, 127, 1))
        planes.append(plane)
        slopes.append(upper - lower)
        sums.append(upper + lower)
    for x in range(1, 5):
        fibre = fibre_ref[x - 1]

        def coef(row):
            value = jnp.full((16, 128), coef_ref[row * REGIONS])
            for r in range(1, REGIONS):
                value = jnp.where(fibre == r, coef_ref[row * REGIONS + r], value)
            return value

        here, left, right = planes[x], planes[x - 1], planes[x + 1]
        centre = here[1:17]
        twice = 2.0 * centre
        total = coef(0) * (right[1:17] + left[1:17] - twice)
        total = total + coef(1) * (here[2:18] + here[0:16] - twice)
        total = total + coef(2) * (sums[x][1:17] - twice)
        total = total + 0.5 * coef(3) * (right[2:18] - right[0:16] - left[2:18] + left[0:16])
        total = total + 0.5 * coef(4) * (slopes[x + 1][1:17] - slopes[x - 1][1:17])
        total = total + 0.5 * coef(5) * (slopes[x][2:18] - slopes[x][0:16])
        out_ref[16 * (x - 1) : 16 * x, :] = centre + total


def diffuse_kernel(plan_ref, coef_ref, planes_ref, before_ref, after_ref, fibre_ref, out_ref, *line_refs):
    stencil(coef_ref, planes_ref, before_ref, after_ref, fibre_ref, out_ref)
    for m, ref in zip(LATE, line_refs):
        p = partner(plan_ref, m)
        for s in range(4):
            ref[s : s + 1, :] = out_ref[pl.ds(plan_ref[p * 4 + s], 1), :]


def home_kernel(tab_ref, states_ref, level_ref, tags_ref, out_ref, current_ref):
    current_ref[...] = react_home(tab_ref, states_ref, level_ref[...], tags_ref[...], out_ref)


def lender_kernel(tab_ref, *refs):
    n = len(LATE)
    messages, lines, outs, hold_ref = refs[:n], refs[n : 2 * n], refs[2 * n : 3 * n], refs[3 * n]
    levels = []
    for ref in lines:
        hold_ref[0:4, :] = ref[...]
        hold_ref[4:8, :] = ref[...]
        levels.append(hold_ref[...])
    for ref, current in zip(outs, react_lent(tab_ref, messages, levels, None)):
        ref[...] = current[0:4, :]


def early_kernel(plan_ref, tab_ref, level_ref, current_ref, *refs):
    messages, out_ref, fresh, hold_ref = refs[:SOON], refs[SOON], refs[SOON + 1 : 2 * SOON + 1], refs[-1]
    out_ref[...] = current_ref[...]
    levels = [gather_lines(plan_ref, m, level_ref, hold_ref) for m in EARLY[:SOON]]
    currents = react_lent(tab_ref, messages, levels, fresh)
    for m, value in zip(EARLY[:SOON], currents):
        put_lines(plan_ref, m, hold_ref, value, out_ref)


def first_kernel(plan_ref, tab_ref, level_ref, current_ref, *refs):
    rest = EARLY[SOON:]
    n, l = len(rest), len(LATE)
    messages, lent = refs[:n], refs[n : n + l]
    out_ref, fresh = refs[n + l], refs[n + l + 1 : 2 * n + l + 1]
    hold_ref, sum_ref = refs[2 * n + l + 1 :]
    sum_ref[...] = current_ref[...]
    levels = [gather_lines(plan_ref, m, level_ref, hold_ref) for m in rest]
    currents = react_lent(tab_ref, messages, levels, fresh)
    for m, value in zip(rest, currents):
        put_lines(plan_ref, m, hold_ref, value, sum_ref)
    for m, ref in zip(LATE, lent):
        hold_ref[0:4, :] = ref[...]
        put_lines(plan_ref, m, hold_ref, hold_ref[...], sum_ref)
    out_ref[...] = level_ref[...] - 0.25 * sum_ref[...]


def second_kernel(plan_ref, tab_ref, coef_ref, planes_ref, before_ref, after_ref, fibre_ref, first_ref, states_ref, tags_ref, *refs):
    n, l = len(EARLY), len(LATE)
    early, late = refs[:n], refs[n : n + l]
    volt_ref, out_ref, hold_ref, level_ref, sum_ref = refs[n + l : n + l + 5]
    fresh = refs[n + l + 5 :]
    levels = [gather_lines(plan_ref, m, first_ref, hold_ref) for m in LATE]
    react_lent(tab_ref, late, levels, fresh[n:])
    stencil(coef_ref, planes_ref, before_ref, after_ref, fibre_ref, level_ref)
    sum_ref[...] = react_home(tab_ref, states_ref, level_ref[...], tags_ref[...], out_ref)
    levels = [gather_lines(plan_ref, m, level_ref, hold_ref) for m in EARLY + LATE]
    currents = react_lent(tab_ref, (*early, *fresh[n:]), levels, fresh)
    for m, value, ref in zip(EARLY + LATE, currents, fresh):
        put_lines(plan_ref, m, hold_ref, value, sum_ref)
        put_states(plan_ref, m, ref, out_ref)
    volt_ref[...] = level_ref[...] - 0.25 * sum_ref[...]


def call(body, outs, ins, scratch=(), flops=0, **kwargs):
    size = sum(4 * v.size for v in ins) + sum(4 * v.size for v in outs)
    return pl.pallas_call(
        body,
        out_shape=tuple(outs),
        in_specs=[SMEM if v.ndim == 1 else VMEM for v in ins],
        out_specs=tuple(VMEM for _ in outs),
        scratch_shapes=[pltpu.VMEM(s, jnp.float32) for s in scratch],
        compiler_params=pltpu.CompilerParams(vmem_limit_bytes=32 * 1024 * 1024),
        cost_estimate=pl.CostEstimate(flops=flops, bytes_accessed=size, transcendentals=0),
        **kwargs,
    )(*ins)


def shift(value, axis):
    peers = lax.axis_size(axis)
    return (
        lax.ppermute(value[0], axis, [(i, i + 1) for i in range(peers - 1)]),
        lax.ppermute(value[1], axis, [(i + 1, i) for i in range(peers - 1)]),
    )


def beside_depth(field):
    place, peers = lax.axis_index("depth"), lax.axis_size("depth")
    layers = lax.all_gather(jnp.concatenate([field[:1], field[-1:]], axis=0), "depth")
    lower = lax.dynamic_index_in_dim(layers, jnp.maximum(place - 1, 0), 0, keepdims=False)
    upper = lax.dynamic_index_in_dim(layers, jnp.minimum(place + 1, peers - 1), 0, keepdims=False)
    return jnp.where(place > 0, lower[1:], 0.0), jnp.where(place < peers - 1, upper[:1], 0.0)


def halo_depth_last(field, send):
    send("rows", field)
    before, after = shift((field[:, -1:], field[:, :1]), "rows")
    field = jnp.concatenate([before, field, after], axis=1)
    before, after = shift((field[:, :, 127], field[:, :, 0]), "cols")
    count = field.shape[1]

    def face(x):
        columns = jnp.pad(jnp.stack([before[x], after[x]]), ((0, 4), (0, 128 - count)))
        return jnp.concatenate([field[x], columns], axis=0)

    place, peers = lax.axis_index("depth"), lax.axis_size("depth")
    layers = lax.all_gather(jnp.stack([face(0), face(-1)]), "depth")
    lower = lax.dynamic_index_in_dim(layers, jnp.maximum(place - 1, 0), 0, keepdims=False)[1:]
    upper = lax.dynamic_index_in_dim(layers, jnp.minimum(place + 1, peers - 1), 0, keepdims=False)[:1]
    lower, upper = jnp.where(place > 0, lower, 0.0), jnp.where(place < peers - 1, upper, 0.0)
    field = jnp.concatenate([lower[:, :count], field, upper[:, :count]], axis=0)
    before = jnp.concatenate([lower[:, count, :count], before, upper[:, count, :count]], axis=0)
    after = jnp.concatenate([lower[:, count + 1, :count], after, upper[:, count + 1, :count]], axis=0)
    return field, before[..., None], after[..., None]


def halo(field, send=lambda phase, *after: ()):
    field = tied(field, *send("depth", field))
    before, after = beside_depth(field)
    field = jnp.concatenate([before, field, after], axis=0)
    field = tied(field, *send("rows", field))
    before, after = shift((field[:, -1:], field[:, :1]), "rows")
    field = jnp.concatenate([before, field, after], axis=1)
    field = tied(field, *send("cols", field))
    before, after = shift((field[:, :, 127], field[:, :, 0]), "cols")
    return field, before[..., None], after[..., None]


def tied(value, *others):
    if not others:
        return value
    return lax.optimization_barrier((value, *others))[0]


def local(
    voltage,
    states,
    cell_tags,
    fibre_ids,
    loan_states,
    loan_tags,
    lend_block,
    lend_count,
    diffuse_main,
    diffuse_cross,
    gate_half,
    gate_slope,
    gate_rate,
    conductance,
    reversal,
):
    line = (BLOCKS, 128)
    own = lax.axis_index("cols") % HALF
    plan = jnp.concatenate([lend_block.reshape(-1), lend_count.reshape(-1), own[None].astype(jnp.int32)])
    table = jnp.concatenate(
        [t.reshape(-1) for t in (gate_half, 0.5 / gate_slope, -gate_rate, conductance, reversal)]
    )
    coef = jnp.concatenate([diffuse_main.reshape(-1), diffuse_cross.reshape(-1)])
    home = states.transpose(0, 2, 1, 3).reshape(4 * STATES * 16, 128)
    tags = cell_tags.reshape(line)

    held = loan_states[0].transpose(0, 2, 1, 3)
    message = {}
    for m in EARLY + LATE:
        source = jnp.bitwise_xor(own, m)
        body = lax.dynamic_index_in_dim(held, source, 0, keepdims=False).reshape(STATES * 4, 128)
        kinds = lax.dynamic_index_in_dim(loan_tags[0], source, 0, keepdims=False)
        message[m] = jnp.concatenate([body, kinds.astype(jnp.float32)], axis=0)

    got = {}

    def send(m, *after):
        got[m] = lax.ppermute(tied(message[m], *after), "cols", to_heavy(m))

    e0, e1, e2, e3, e4, e5 = EARLY
    send(e0)
    send(e1)
    send(e2)

    def beside(phase, field):
        if phase == "depth":
            return message[e0], message[e1], message[e2]
        if phase == "cols":
            send(e3, field, got[e0])
            return (got[e0],)
        return ()

    diffused, *lines = call(
        diffuse_kernel,
        [f32(*line)] + [f32(4, 128) for _ in LATE],
        [plan, coef, *halo(voltage, beside), fibre_ids],
    )
    send(e4, diffused, got[e1])
    send(e5, diffused, got[e2])
    lines = [lax.ppermute(tied(v, got[e1], got[e2]), "cols", to_light(m)) for m, v in zip(LATE, lines)]
    back = call(
        lender_kernel,
        [f32(4, 128) for _ in LATE],
        [table, *(message[m] for m in LATE), *lines],
        scratch=[(8, 128)],
    )
    first, current = call(
        home_kernel, [f32(*home.shape), f32(*line)], [table, home, tied(diffused, *back), tags]
    )
    back = [lax.ppermute(v, "cols", to_heavy(m)) for m, v in zip(LATE, back)]
    current, *fresh = call(
        early_kernel,
        [f32(*line)] + [f32(ROWS, 128) for _ in EARLY[:SOON]],
        [plan, table, diffused, current, *(got[m] for m in EARLY[:SOON])],
        scratch=[(8, 128)],
    )
    volt, *others = call(
        first_kernel,
        [f32(*line)] + [f32(ROWS, 128) for _ in EARLY[SOON:]],
        [plan, table, diffused, current, *(got[m] for m in EARLY[SOON:]), *back],
        scratch=[(8, 128), line],
    )
    fresh += others

    def beside_second(phase, field):
        for m in LATE:
            send(m, field)

    planes = halo_depth_last(volt.reshape(4, 16, 128), beside_second)
    late = [got[m] for m in LATE]
    volt, out = call(
        second_kernel,
        [f32(*line), f32(*home.shape)],
        [plan, table, coef, *planes, fibre_ids, diffused, first, tags, *fresh, *late],
        scratch=[(8, 128), line, line] + [(ROWS, 128) for _ in EARLY + LATE],
    )
    return volt.reshape(4, 16, 128), out.reshape(4, STATES, 16, 128).transpose(0, 2, 1, 3)


def solution(mesh):
    brick = P("depth", "rows", "cols")
    every = ("depth", "rows", "cols")
    in_specs = (
        brick,
        P("depth", "rows", None, "cols"),
        brick,
        brick,
        P(every, None, None, None, None),
        P(every, None, None, None),
        P(every, None, None),
        P(every, None),
    ) + (P(),) * 7
    out_specs = (brick, P("depth", "rows", None, "cols"))
    return jax.shard_map(local, mesh=mesh, in_specs=in_specs, out_specs=out_specs, check_vma=False)
```
